32 devices in a mesh: dp: 4 (over x, core), seq: 8 (over z, y).
Axes of the slice: x: 2, y: 2, z: 4, core: 2. Of those that a mesh axis runs over, the one named last changes fastest.
Arguments:
- queries: bfloat16 [4, 2048, 2048], P('dp', 'seq'), may hold values from -8 to 8
- key_states: bfloat16 [4, 2048, 512], P('dp', 'seq'), may hold values from -6 to 6
- value_states: bfloat16 [4, 2048, 512], P('dp', 'seq'), may hold values from -6 to 6
- block_picks: int32 [4, 3, 8], P('dp'), may hold values from 0 to 1
- out_weight: bfloat16 [2048, 2048], P(('dp', 'seq')), may hold values from -0.5 to 0.5
- out_grad: bfloat16 [4, 2048, 2048], P('dp', 'seq'), may hold values from -4 to 4
Outputs:
- layer_out: bfloat16 [4, 2048, 2048], P('dp', 'seq')
- query_grad: bfloat16 [4, 2048, 2048], P('dp', 'seq')
- key_grad: bfloat16 [4, 2048, 512], P('dp', 'seq')
- value_grad: bfloat16 [4, 2048, 512], P('dp', 'seq')
The draws below stay inside these ranges and needn't reach their ends.
All inputs are finite; a program needn't handle non-finite values.
Results may differ from the reference program's by a relative error of at most 0.025.
Values may be sent and summed in bfloat16 or wider, within the bound.
A program may use at most 128 MiB of HBM per device.

```python
import math
import jax
import jax.numpy as jnp
from jax import lax

KV_HEADS = 4
HEAD_DIM = 128
OUT_WIDTH = 2048
BLOCK = 128
TOK_DEV = 256
GROUP = 4
Q_WIDTH = 2048
KV_WIDTH = 512
BLOCKS_DEV = 2
LEVELS = 3
SEQS = 4
SEQ_LEN = 2048
KEY_COUNT = 640
N_SEQ = 8


def draw_queries(key, part):
    own_key = jax.random.fold_in(key, 23)
    shape = (SEQS, SEQ_LEN, Q_WIDTH)
    return jnp.clip(1.25 * jax.random.normal(own_key, shape, jnp.float32), -6.0, 6.0).astype(jnp.bfloat16)


def draw_key_states(key, part):
    own_key = jax.random.fold_in(key, 37)
    shape = (SEQS, SEQ_LEN, KV_WIDTH)
    return jnp.clip(1.2 * jax.random.normal(own_key, shape, jnp.float32), -6.0, 6.0).astype(jnp.bfloat16)


def plant(entries, key, least, top_value):
    longest = entries.shape.index(max(entries.shape))
    spots = []
    for shift in (0, 1):
        where = [jax.random.randint(jax.random.fold_in(key, axis), (), 0, length) for axis, length in enumerate(entries.shape)]
        where[longest] = (where[longest] + shift) % entries.shape[longest]
        spots.append(tuple(where))
    return entries.at[spots[0]].set(least).at[spots[1]].set(top_value)


def block_scale(rng, shape, cuts, least, top_value):
    gain = 1.0
    for dim, parts in cuts:
        draws = jax.random.uniform(jax.random.fold_in(jax.random.fold_in(rng, 6), dim), (parts,), jnp.float32, least / len(cuts), top_value / len(cuts))
        gain = gain * jnp.repeat(jnp.exp(draws), shape[dim] // parts).reshape((-1,) + (1,) * (len(shape) - 1 - dim))
    return gain


def centred(rng, extent, width, bound, cuts=(), held_as=jnp.bfloat16):
    drawn = jax.random.normal(rng, extent, jnp.float32) * width
    if len(cuts) > 0:
        drawn = block_scale(rng, extent, cuts, -0.22, 0.18) * drawn
    return jnp.clip(drawn, min=-bound, max=bound).astype(held_as)


def setup_inputs(seed: int = 0) -> dict:
    splits = jax.random.split(jax.random.key(seed), 7)
    return {
        "queries": draw_queries(jax.random.fold_in(splits[6], 71), 0),
        "key_states": draw_key_states(jax.random.fold_in(splits[6], 71), 0),
        "value_states": centred(splits[2], (SEQS, SEQ_LEN, KV_WIDTH), 1.0, 6.0, ((0, 4), (1, 8))),
        "block_picks": plant(jax.random.randint(splits[3], (SEQS, LEVELS, N_SEQ), 0, BLOCKS_DEV), jax.random.fold_in(splits[3], 1), 0, BLOCKS_DEV - 1).astype(jnp.int32),
        "out_weight": centred(splits[4], (Q_WIDTH, OUT_WIDTH), (Q_WIDTH // 16) ** -0.5, 0.5, ((0, 32),)),
        "out_grad": centred(splits[5], (SEQS, SEQ_LEN, OUT_WIDTH), 0.25, 4.0, ((0, 4), (1, 8))),
    }


neg_fill = -1e+30

def key_positions(picks_one):
    shard_ids = jnp.arange(N_SEQ, dtype=jnp.int32)
    offsets = jnp.arange(TOK_DEV, dtype=jnp.int32)
    pieces = [shard_ids[:, None] * TOK_DEV + offsets[None, :]]
    seen_parts = [jnp.ones((N_SEQ, TOK_DEV), dtype=jnp.bool_)]
    for level_index in range(LEVELS):
        distance = 2 ** level_index
        source = jnp.maximum(shard_ids - distance, 0)
        block_ids = source * BLOCKS_DEV + picks_one[level_index].astype(jnp.int32)
        pieces.append(block_ids[:, None] * BLOCK + jnp.arange(BLOCK, dtype=jnp.int32)[None, :])
        seen_parts.append(jnp.broadcast_to((shard_ids >= distance)[:, None], (N_SEQ, BLOCK)))
    return (jnp.concatenate(pieces, 1), jnp.concatenate(seen_parts, 1))

def shard_terms(query_shard, key_seq, value_seq, positions, seen, grad_shard, scale_value):
    key_rows = key_seq[positions].astype(jnp.float32).reshape(KEY_COUNT, KV_HEADS, HEAD_DIM)
    value_rows = value_seq[positions].astype(jnp.float32).reshape(KEY_COUNT, KV_HEADS, HEAD_DIM)
    query_heads = query_shard.astype(jnp.float32).reshape(TOK_DEV, KV_HEADS, GROUP, HEAD_DIM)
    grad_heads = grad_shard.astype(jnp.float32).reshape(TOK_DEV, KV_HEADS, GROUP, HEAD_DIM)
    row_ids = jnp.arange(TOK_DEV, dtype=jnp.int32)
    col_ids = jnp.arange(KEY_COUNT, dtype=jnp.int32)
    visible = jnp.where(col_ids[None, :] < TOK_DEV, col_ids[None, :] <= row_ids[:, None], seen[None, :])
    scores = jnp.einsum('tkgd,skd->kgts', query_heads, key_rows) * scale_value
    scores = jnp.where(visible[None, None], scores, neg_fill)
    row_max = lax.optimization_barrier(jnp.max(scores, axis=-1, keepdims=True))
    exp_scores = jnp.exp(scores - row_max)
    probs = exp_scores / lax.optimization_barrier(jnp.sum(exp_scores, axis=-1, keepdims=True))
    probs_low = lax.optimization_barrier(probs.astype(jnp.bfloat16)).astype(jnp.float32)
    attn = jnp.einsum('kgts,skd->tkgd', probs_low, value_rows).astype(jnp.bfloat16)
    attn_wide = lax.optimization_barrier(attn).astype(jnp.float32)
    row_delta = jnp.einsum('tkgd,tkgd->kgt', grad_heads, attn_wide)[..., None]
    prob_grad = jnp.einsum('tkgd,skd->kgts', grad_heads, value_rows)
    score_grad = probs * (prob_grad - row_delta)
    score_low = lax.optimization_barrier(score_grad.astype(jnp.bfloat16)).astype(jnp.float32)
    query_grad = (jnp.einsum('kgts,skd->tkgd', score_low, key_rows) * scale_value).astype(jnp.bfloat16)
    key_terms = jnp.einsum('kgts,tkgd->skd', score_low, query_heads) * scale_value
    value_terms = jnp.einsum('kgts,tkgd->skd', probs_low, grad_heads)
    return (attn.reshape(TOK_DEV, Q_WIDTH), query_grad.reshape(TOK_DEV, Q_WIDTH), key_terms.reshape(KEY_COUNT, KV_WIDTH), value_terms.reshape(KEY_COUNT, KV_WIDTH))

def reference(queries, key_states, value_states, block_picks, out_weight, out_grad):
    scale_value = 1.0 / math.sqrt(HEAD_DIM)

    def one_sequence(items):
        query_seq, key_seq, value_seq, picks_one, grad_seq = items
        positions, seen = key_positions(picks_one)
        attn_grad = jnp.dot(grad_seq, out_weight.T, preferred_element_type=jnp.float32).astype(jnp.bfloat16)

        def one_shard(shard_items):
            query_shard, shard_pos, shard_seen, grad_shard = shard_items
            return shard_terms(query_shard, key_seq, value_seq, shard_pos, shard_seen, grad_shard, scale_value)
        attn, query_grad, key_terms, value_terms = lax.map(one_shard, (query_seq.reshape(N_SEQ, TOK_DEV, Q_WIDTH), positions, seen, attn_grad.reshape(N_SEQ, TOK_DEV, Q_WIDTH)))
        attn = attn.reshape(SEQ_LEN, Q_WIDTH)
        layer_out = jnp.dot(attn, out_weight, preferred_element_type=jnp.float32).astype(jnp.bfloat16)
        flat_pos = positions.reshape(-1)
        key_grad = jnp.zeros((SEQ_LEN, KV_WIDTH), jnp.float32).at[flat_pos].add(key_terms.reshape(-1, KV_WIDTH)).astype(jnp.bfloat16)
        value_grad = jnp.zeros((SEQ_LEN, KV_WIDTH), jnp.float32).at[flat_pos].add(value_terms.reshape(-1, KV_WIDTH)).astype(jnp.bfloat16)
        return (layer_out, query_grad.reshape(SEQ_LEN, Q_WIDTH), key_grad, value_grad)
    layer_out, query_grad, key_grad, value_grad = lax.map(one_sequence, (queries, key_states, value_states, block_picks, out_grad))
    return (layer_out, query_grad, key_grad, value_grad)
```

```python
import math

import jax
import jax.numpy as jnp
from jax import lax
from jax.experimental import pallas as pl
from jax.experimental.pallas import tpu as pltpu
from jax.sharding import PartitionSpec as P

HEAD_DIM = 128
BLOCK = 128


neg_fill = -1e30


def shifted(block, axis, distance):
    devices = range(lax.axis_size(axis))
    route = [(i - distance, i) for i in devices if i - distance in devices]
    return lax.ppermute(block, axis, route)


def shards(queries, key_states, value_states, block_picks, out_weight, out_grad):
    query_rows = queries[0]
    key_rows = key_states[0]
    value_rows = value_states[0]
    grad_rows = out_grad[0]
    picks_here = block_picks[0]
    tok_count = query_rows.shape[0]
    q_cols = query_rows.shape[1]
    kv_cols = key_rows.shape[1]
    kv_count = kv_cols // HEAD_DIM
    group_size = q_cols // kv_cols
    score_scale = 1.0 / math.sqrt(HEAD_DIM)
    seq_count = lax.axis_size("seq")
    level_count = seq_count.bit_length() - 1
    shard_index = lax.axis_index("seq")
    far_keys = []
    far_values = []
    for level_index in range(level_count):
        distance = 1 << level_index
        got_keys, got_values = shifted((key_rows, value_rows), "seq", distance)
        row_begin = picks_here[level_index, shard_index] * BLOCK
        far_keys.append(lax.dynamic_slice_in_dim(got_keys, row_begin, BLOCK, 0))
        far_values.append(lax.dynamic_slice_in_dim(got_values, row_begin, BLOCK, 0))
    all_keys = jnp.concatenate([key_rows] + far_keys, 0)
    all_values = jnp.concatenate([value_rows] + far_values, 0)
    key_total = all_keys.shape[0]
    row_ids = lax.broadcasted_iota(jnp.int32, (tok_count, key_total), 0)
    col_ids = lax.broadcasted_iota(jnp.int32, (tok_count, key_total), 1)
    far_level = jnp.maximum(col_ids - tok_count, 0) // BLOCK
    far_seen = shard_index >= jnp.left_shift(jnp.int32(1), far_level)
    visible = jnp.where(col_ids < tok_count, col_ids <= row_ids, far_seen)
    whole_weight = lax.all_gather(out_weight, ("dp", "seq"), axis=0, tiled=True)
    attn_grad = lax.dot_general(
        grad_rows, whole_weight, (((1,), (1,)), ((), ())), preferred_element_type=jnp.float32
    )
    attn_grad = attn_grad.astype(jnp.bfloat16)
    query_heads = query_rows.reshape(tok_count, kv_count, group_size, HEAD_DIM)
    key_heads = all_keys.reshape(key_total, kv_count, HEAD_DIM)
    value_heads = all_values.reshape(key_total, kv_count, HEAD_DIM)
    grad_heads = attn_grad.reshape(tok_count, kv_count, group_size, HEAD_DIM)
    attn_parts = []
    dq_parts = []
    dk_parts = []
    dv_parts = []
    for group_index in range(kv_count):
        query_group = query_heads[:, group_index]
        key_group = key_heads[:, group_index]
        value_group = value_heads[:, group_index]
        grad_group = grad_heads[:, group_index]
        scores = (
            jnp.einsum("tgd,sd->gts", query_group, key_group, preferred_element_type=jnp.float32)
            * score_scale
        )
        scores = jnp.where(visible[None], scores, neg_fill)
        row_max = jnp.max(scores, axis=-1, keepdims=True)
        exp_scores = jnp.exp(scores - row_max)
        probs = exp_scores / jnp.sum(exp_scores, axis=-1, keepdims=True)
        probs_low = probs.astype(jnp.bfloat16)
        attn_group = jnp.einsum(
            "gts,sd->tgd", probs_low, value_group, preferred_element_type=jnp.float32
        ).astype(jnp.bfloat16)
        row_delta = jnp.einsum(
            "tgd,tgd->gt", grad_group, attn_group, preferred_element_type=jnp.float32
        )[:, :, None]
        prob_grad = jnp.einsum(
            "tgd,sd->gts", grad_group, value_group, preferred_element_type=jnp.float32
        )
        score_low = (probs * (prob_grad - row_delta)).astype(jnp.bfloat16)
        dq_parts.append(
            (
                jnp.einsum("gts,sd->tgd", score_low, key_group, preferred_element_type=jnp.float32)
                * score_scale
            ).astype(jnp.bfloat16)
        )
        dk_parts.append(
            jnp.einsum("gts,tgd->sd", score_low, query_group, preferred_element_type=jnp.float32)
            * score_scale
        )
        dv_parts.append(
            jnp.einsum("gts,tgd->sd", probs_low, grad_group, preferred_element_type=jnp.float32)
        )
        attn_parts.append(attn_group)
    attn_all = jnp.stack(attn_parts, 1).reshape(tok_count, q_cols)
    query_grad = jnp.stack(dq_parts, 1).reshape(tok_count, q_cols)
    key_terms = jnp.stack(dk_parts, 1).reshape(key_total, kv_cols)
    value_terms = jnp.stack(dv_parts, 1).reshape(key_total, kv_cols)
    layer_sum = jnp.dot(attn_all, whole_weight, preferred_element_type=jnp.float32)
    layer_out = layer_sum.astype(jnp.bfloat16)
    key_grad = key_terms[:tok_count]
    value_grad = value_terms[:tok_count]
    for level_index in range(level_count):
        distance = 1 << level_index
        begin = tok_count + level_index * BLOCK
        back_keys, back_values = shifted(
            (key_terms[begin : begin + BLOCK], value_terms[begin : begin + BLOCK]), "seq", -distance
        )
        source = jnp.minimum(shard_index + distance, seq_count - 1)
        row_begin = picks_here[level_index, source] * BLOCK
        key_grad = lax.dynamic_update_slice_in_dim(
            key_grad,
            lax.dynamic_slice_in_dim(key_grad, row_begin, BLOCK, 0) + back_keys,
            row_begin,
            0,
        )
        value_grad = lax.dynamic_update_slice_in_dim(
            value_grad,
            lax.dynamic_slice_in_dim(value_grad, row_begin, BLOCK, 0) + back_values,
            row_begin,
            0,
        )
    return (
        layer_out[None],
        query_grad[None],
        key_grad.astype(jnp.bfloat16)[None],
        value_grad.astype(jnp.bfloat16)[None],
    )


MESH = pl.DeviceIdType.MESH
NT = (((1,), (1,)), ((), ()))
NN = (((1,), (0,)), ((), ()))
TN = (((0,), (0,)), ((), ()))


def dot(a, b, dims):
    return lax.dot_general(a, b, dims, preferred_element_type=jnp.float32)


def fused_kernel(
    picks, q_hbm, k_in, v_in, w_in, og_hbm,
    lo_out, dq_out, dk_out, dv_out,
    q_v, og_v, wbuf, kall, vall, k_t, v_t, kv_stage, probs, attn_t, lo_acc,
    dk_acc, dv_acc, gr_stage, gr_in,
    in_sem, kv_ssem, kv_rsem, z_ssem, x_ssem, y_ssem, s_ssem, xh_ssem, yh_ssem,
    z_rsem, x_rsem, y_rsem, s_rsem, xh_rsem, yh_rsem, gr_ssem, gr_rsem,
):
    dp = lax.axis_index("dp")
    seq = lax.axis_index("seq")
    n_seq = lax.axis_size("seq")
    n_z = n_seq // 2
    x, core = dp // 2, dp % 2
    z, y = seq // 2, seq % 2
    rows = w_in.shape[0]
    half = rows // 2
    tok = q_v.shape[0]
    group_rows = rows * n_seq
    pair_rows = group_rows // 2
    heads = q_v.shape[1] // HEAD_DIM
    kv_heads = k_in.shape[1] // HEAD_DIM
    group_size = heads // kv_heads
    pair_heads = group_size // 2
    levels = n_seq.bit_length() - 1
    scale = 1.0 / math.sqrt(HEAD_DIM)
    log2_scale = scale * math.log2(math.e)

    sib = (x * 2 + 1 - core, seq)
    xn = ((1 - x) * 2 + core, seq)
    yn = (dp, z * 2 + 1 - y)
    d_own, d_sib, d_x, d_xs = dp, sib[0], xn[0], (1 - x) * 2 + 1 - core

    q_copy = pltpu.make_async_copy(q_hbm, q_v, in_sem.at[0])
    og_copy = pltpu.make_async_copy(og_hbm, og_v, in_sem.at[1])
    q_copy.start()
    og_copy.start()

    barrier = pltpu.get_barrier_semaphore()
    count = jnp.int32(2)
    for dev in (sib, xn):
        pl.semaphore_signal(barrier, inc=1, device_id=dev, device_id_type=MESH)
    for j in range(levels):
        dist = 1 << j

        @pl.when(seq + dist < n_seq)
        def _():
            pl.semaphore_signal(barrier, inc=1, device_id=(dp, seq + dist), device_id_type=MESH)

        @pl.when(seq >= dist)
        def _():
            pl.semaphore_signal(barrier, inc=1, device_id=(dp, seq - dist), device_id_type=MESH)

        count += (seq + dist < n_seq).astype(jnp.int32) + (seq >= dist).astype(jnp.int32)

    def w_row(d, zz, yy):
        return pl.multiple_of((d * n_seq + zz * 2 + yy) * rows, rows)

    def w_at(d, zz, yy):
        return wbuf.at[pl.ds(w_row(d, zz, yy), rows)]

    def w_half(d, zz, yy, hf):
        return wbuf.at[pl.ds(pl.multiple_of(w_row(d, zz, yy) + hf * half, half), half)]

    for j in range(levels):
        target = jnp.minimum(seq + (1 << j), n_seq - 1)
        second = picks[0, j, target].astype(jnp.float32)
        for i, buf in enumerate((k_in, v_in)):
            first_rows = buf[0:BLOCK, :].astype(jnp.float32) * (1.0 - second)
            second_rows = buf[BLOCK : 2 * BLOCK, :].astype(jnp.float32) * second
            kv_stage[j, i] = (first_rows + second_rows).astype(jnp.bfloat16)
    wbuf[pl.ds(w_row(dp, z, y), rows), :] = w_in[...]
    kall[0:tok, :] = k_in[...]
    vall[0:tok, :] = v_in[...]
    pl.semaphore_wait(barrier, count)

    def remote(src, dst, ssem, rsem, dev):
        return pltpu.make_async_remote_copy(
            src_ref=src, dst_ref=dst, send_sem=ssem, recv_sem=rsem, device_id=dev, device_id_type=MESH
        )

    def kv_copies(j):
        out = []
        for i, buf in enumerate((kall, vall)):
            dst = buf.at[pl.ds(tok + j * BLOCK, BLOCK)]
            dev = (dp, jnp.minimum(seq + (1 << j), n_seq - 1))
            out.append(remote(kv_stage.at[j, i], dst, kv_ssem.at[j, i], kv_rsem.at[j, i], dev))
        return out

    z_order = (z, jnp.bitwise_xor(z, 1), jnp.where(z < 2, 2, 1), jnp.where(z < 2, 3, 0))

    def z_copy(zz, up):
        dev = (dp, seq + 2) if up else (dp, seq - 2)
        return remote(w_at(dp, zz, y), w_at(dp, zz, y), z_ssem.at[int(up), zz], z_rsem.at[zz], dev)

    def x_copy(zz, d):
        return remote(w_at(d, zz, y), w_at(d, zz, y), x_ssem.at[zz], x_rsem.at[zz], xn)

    def y_copy(zz, yy):
        return remote(w_at(dp, zz, yy), w_at(dp, zz, yy), y_ssem.at[zz], y_rsem.at[zz], yn)

    def xh_copy(zz, d):
        piece = w_half(d, zz, 1 - y, 1)
        return remote(piece, piece, xh_ssem.at[zz], xh_rsem.at[zz], xn)

    def yh_copy(zz, yy):
        piece = w_half(d_x, zz, yy, 0)
        return remote(piece, piece, yh_ssem.at[zz], yh_rsem.at[zz], yn)

    def s_copy(zz, kind, other):
        d = (d_x if kind & 1 else d_own) if not other else (d_xs if kind & 1 else d_sib)
        yy = 1 - y if kind & 2 else y
        piece = w_at(d, zz, yy)
        return remote(piece, piece, s_ssem.at[kind, zz], s_rsem.at[kind, zz], sib)

    def z_sends(zz, act):
        @pl.when(jnp.logical_and(zz <= z, z < n_z - 1))
        def _():
            act(z_copy(zz, True))

        @pl.when(jnp.logical_and(zz >= z, z > 0))
        def _():
            act(z_copy(zz, False))

    def start(c):
        c.start()

    def own_event(i):
        zz = z_order[i]
        if i:
            z_copy(zz, True).wait_recv()
        z_sends(zz, start)
        x_copy(zz, d_own).start()
        y_copy(zz, y).start()
        s_copy(zz, 0, False).start()

    def xy_event(i):
        zz = z_order[i]
        x_copy(zz, d_x).wait_recv()
        yh_copy(zz, y).start()
        s_copy(zz, 1, False).start()
        y_copy(zz, 1 - y).wait_recv()
        xh_copy(zz, d_own).start()
        s_copy(zz, 2, False).start()

    def diag_event(i):
        zz = z_order[i]
        yh_copy(zz, 1 - y).wait_recv()
        xh_copy(zz, d_x).wait_recv()
        s_copy(zz, 3, False).start()

    def sib_wait(i, kinds):
        for kind in kinds:
            s_copy(z_order[i], kind, True).wait_recv()

    for j in range(levels):
        @pl.when(seq + (1 << j) < n_seq)
        def _():
            for c in kv_copies(j):
                c.start()

    own_event(0)

    for j in range(levels):
        @pl.when(seq < (1 << j))
        def _():
            for buf in (kall, vall):
                buf[tok + j * BLOCK : tok + (j + 1) * BLOCK, :] = jnp.zeros((BLOCK, buf.shape[1]), buf.dtype)

    dk_acc[...] = jnp.zeros_like(dk_acc)
    dv_acc[...] = jnp.zeros_like(dv_acc)
    lo_acc[...] = jnp.zeros_like(lo_acc)
    q_copy.wait()
    for j in range(levels):
        @pl.when(seq >= (1 << j))
        def _():
            for c in kv_copies(j):
                c.wait_recv()

    def group_cols(g):
        return pl.ds(pl.multiple_of(g * HEAD_DIM, HEAD_DIM), HEAD_DIM)

    causal = lax.broadcasted_iota(jnp.int32, (tok, tok), 0) <= lax.broadcasted_iota(jnp.int32, (tok, tok), 1)

    def softmax_head(h, carry):
        g = h // group_size
        s = dot(kall[:, group_cols(g)], q_v[:, group_cols(h)], NT)
        parts = [jnp.where(causal, s[:tok], neg_fill)]
        for j in range(levels):
            bias = jnp.where(seq >= (1 << j), 0.0, neg_fill).astype(jnp.float32)
            parts.append(s[tok + j * BLOCK : tok + (j + 1) * BLOCK] + bias)
        top = jnp.max(parts[0], axis=0, keepdims=True)
        for part in parts[1:]:
            top = jnp.maximum(top, jnp.max(part, axis=0, keepdims=True))
        exps = [jnp.exp2((part - top) * log2_scale) for part in parts]
        total = jnp.sum(exps[0], axis=0, keepdims=True)
        for part in exps[1:]:
            total = total + jnp.sum(part, axis=0, keepdims=True)
        inv = 1.0 / total
        low = jnp.concatenate([(part * inv).astype(jnp.bfloat16) for part in exps], 0)
        probs[h] = low
        at = dot(v_t[group_cols(g), :], low, NN)
        attn_t[pl.ds(pl.multiple_of(h * HEAD_DIM, HEAD_DIM), HEAD_DIM), :] = at.astype(jnp.bfloat16)
        return carry

    k_t[...] = kall[...].T
    v_t[...] = vall[...].T

    def softmaxes(lo, hi):
        lax.fori_loop(lo, hi, softmax_head, 0)

    def unit(g, p):
        base = pl.multiple_of(g * group_rows + p * pair_rows, pair_rows)
        wp = wbuf[pl.ds(base, pair_rows), :]
        g_t = dot(wp, og_v[...], NT).astype(jnp.bfloat16)
        a_t = attn_t[pl.ds(base, pair_rows), :]
        lo_acc[...] += dot(a_t, wp, TN)
        cols = group_cols(g)
        dk = dk_acc[g]
        dv = dv_acc[g]
        for i in range(pair_heads):
            h = g * group_size + p * pair_heads + i
            gh = g_t[i * HEAD_DIM : (i + 1) * HEAD_DIM]
            ah = a_t[i * HEAD_DIM : (i + 1) * HEAD_DIM]
            delta = jnp.sum(gh.astype(jnp.float32) * ah.astype(jnp.float32), axis=0, keepdims=True)
            low = probs[h]
            dprob = dot(vall[:, cols], gh, NN)
            ds = (low.astype(jnp.float32) * (dprob - delta)).astype(jnp.bfloat16)
            dq_t = dot(k_t[cols, :], ds, NN) * scale
            dq_out[:, group_cols(h)] = dq_t.T.astype(jnp.bfloat16)
            dk += dot(ds, q_v[:, group_cols(h)], NN)
            dv += dot(low, gh, NT)
        dk_acc[g] = dk
        dv_acc[g] = dv

    def gr_copy(g, j, back):
        dev = (dp, jnp.maximum(seq - (1 << j), 0))
        return remote(gr_stage.at[g, j], gr_in.at[g, j], gr_ssem.at[g, j], gr_rsem.at[g, j], dev)

    def send_grads(g):
        for j in range(levels):
            @pl.when(seq >= (1 << j))
            def _():
                begin = tok + j * BLOCK
                gr_stage[g, j, 0] = (dk_acc[g, begin : begin + BLOCK, :] * scale).astype(jnp.bfloat16)
                gr_stage[g, j, 1] = dv_acc[g, begin : begin + BLOCK, :].astype(jnp.bfloat16)
                gr_copy(g, j, True).start()

    def finish_grads(g):
        cols = group_cols(g)
        for j in range(levels):
            @pl.when(seq + (1 << j) < n_seq)
            def _():
                gr_copy(g, j, True).wait_recv()
                second = picks[0, j, jnp.minimum(seq + (1 << j), n_seq - 1)].astype(jnp.float32)
                for b, here in enumerate((1.0 - second, second)):
                    part = slice(b * BLOCK, (b + 1) * BLOCK)
                    dk_acc[g, part, :] += gr_in[g, j, 0].astype(jnp.float32) * (here * math.sqrt(HEAD_DIM))
                    dv_acc[g, part, :] += gr_in[g, j, 1].astype(jnp.float32) * here

        dk_out[:, cols] = (dk_acc[g, 0:tok, :] * scale).astype(jnp.bfloat16)
        dv_out[:, cols] = dv_acc[g, 0:tok, :].astype(jnp.bfloat16)

    p0 = z // 2
    p1 = 1 - p0
    quarter = heads // 4
    softmaxes(0, quarter)
    own_event(1)
    xy_event(0)
    softmaxes(quarter, 2 * quarter)
    own_event(2)
    xy_event(1)
    diag_event(0)
    softmaxes(2 * quarter, 3 * quarter)
    own_event(3)
    xy_event(2)
    diag_event(1)
    softmaxes(3 * quarter, 4 * quarter)
    og_copy.wait()
    unit(d_own, p0)
    xy_event(3)
    diag_event(2)
    unit(d_x, p0)
    for i in (0, 1):
        sib_wait(i, (0, 2))
    unit(d_sib, p0)
    diag_event(3)
    unit(d_own, p1)
    send_grads(d_own)
    for i in (0, 1):
        sib_wait(i, (1, 3))
    unit(d_xs, p0)
    for i in (2, 3):
        sib_wait(i, (0, 2))
    unit(d_sib, p1)
    send_grads(d_sib)
    unit(d_x, p1)
    send_grads(d_x)
    for i in (2, 3):
        sib_wait(i, (1, 3))
    unit(d_xs, p1)
    send_grads(d_xs)
    lo_out[...] = lo_acc[...].astype(jnp.bfloat16)
    for g in (d_own, d_sib, d_x, d_xs):
        finish_grads(g)

    def done(c):
        c.wait_send()

    for i in range(n_z):
        zz = z_order[i]
        z_sends(zz, done)
        x_copy(zz, d_own).wait_send()
        y_copy(zz, y).wait_send()
        yh_copy(zz, y).wait_send()
        xh_copy(zz, d_own).wait_send()
        for kind in range(4):
            s_copy(zz, kind, False).wait_send()
    for j in range(levels):
        @pl.when(seq + (1 << j) < n_seq)
        def _():
            for c in kv_copies(j):
                c.wait_send()

        @pl.when(seq >= (1 << j))
        def _():
            for g in range(kv_heads):
                gr_copy(g, j, True).wait_send()


def fused_shards(queries, key_states, value_states, block_picks, out_weight, out_grad):
    q, k, v, og = queries[0], key_states[0], value_states[0], out_grad[0]
    tok, q_cols = q.shape
    kv_cols = k.shape[1]
    n_seq = lax.axis_size("seq")
    levels = n_seq.bit_length() - 1
    keys = tok + levels * BLOCK
    heads, kv_heads = q_cols // HEAD_DIM, kv_cols // HEAD_DIM
    out_width = out_weight.shape[1]
    n_z = n_seq // 2
    vmem = pl.BlockSpec(memory_space=pltpu.VMEM)
    hbm = pl.BlockSpec(memory_space=pl.ANY)
    smem = pl.BlockSpec(memory_space=pltpu.SMEM)
    low = jnp.bfloat16
    dma = pltpu.SemaphoreType.DMA
    outs = pl.pallas_call(
        fused_kernel,
        out_shape=(
            jax.ShapeDtypeStruct((tok, out_width), low),
            jax.ShapeDtypeStruct((tok, q_cols), low),
            jax.ShapeDtypeStruct((tok, kv_cols), low),
            jax.ShapeDtypeStruct((tok, kv_cols), low),
        ),
        in_specs=[smem, hbm, vmem, vmem, vmem, hbm],
        out_specs=(vmem, vmem, vmem, vmem),
        scratch_shapes=[
            pltpu.VMEM((tok, q_cols), low),
            pltpu.VMEM((tok, out_width), low),
            pltpu.VMEM((q_cols, out_width), low),
            pltpu.VMEM((keys, kv_cols), low),
            pltpu.VMEM((keys, kv_cols), low),
            pltpu.VMEM((kv_cols, keys), low),
            pltpu.VMEM((kv_cols, keys), low),
            pltpu.VMEM((levels, 2, BLOCK, kv_cols), low),
            pltpu.VMEM((heads, keys, tok), low),
            pltpu.VMEM((q_cols, tok), low),
            pltpu.VMEM((tok, out_width), jnp.float32),
            pltpu.VMEM((kv_heads, keys, HEAD_DIM), jnp.float32),
            pltpu.VMEM((kv_heads, keys, HEAD_DIM), jnp.float32),
            pltpu.VMEM((kv_heads, levels, 2, BLOCK, HEAD_DIM), low),
            pltpu.VMEM((kv_heads, levels, 2, BLOCK, HEAD_DIM), low),
            dma((2,)),
            dma((levels, 2)),
            dma((levels, 2)),
            dma((2, n_z)),
            dma((n_z,)),
            dma((n_z,)),
            dma((4, n_z)),
            dma((n_z,)),
            dma((n_z,)),
            dma((n_z,)),
            dma((n_z,)),
            dma((n_z,)),
            dma((4, n_z)),
            dma((n_z,)),
            dma((n_z,)),
            dma((kv_heads, levels)),
            dma((kv_heads, levels)),
        ],
        compiler_params=pltpu.CompilerParams(
            collective_id=0, has_side_effects=True, vmem_limit_bytes=56 * 1024 * 1024
        ),
    )(block_picks, q, k, v, out_weight, og)
    return tuple(out[None] for out in outs)


def solution(mesh):
    fused = mesh.shape["dp"] == 4 and mesh.shape["seq"] == 8
    return jax.shard_map(
        fused_shards if fused else shards,
        mesh=mesh,
        in_specs=(
            P("dp", "seq", None),
            P("dp", "seq", None),
            P("dp", "seq", None),
            P("dp", None, None),
            P(("dp", "seq"), None),
            P("dp", "seq", None),
        ),
        out_specs=(
            P("dp", "seq", None),
            P("dp", "seq", None),
            P("dp", "seq", None),
            P("dp", "seq", None),
        ),
        check_vma=False,
    )
```

```python
import math

import jax
import jax.numpy as jnp
from jax import lax
from jax.experimental import pallas as pl
from jax.experimental.pallas import tpu as pltpu
from jax.sharding import PartitionSpec as P

HEAD_DIM = 128
BLOCK = 128


neg_fill = -1e30


def shifted(block, axis, distance):
    devices = range(lax.axis_size(axis))
    route = [(i - distance, i) for i in devices if i - distance in devices]
    return lax.ppermute(block, axis, route)


def shards(queries, key_states, value_states, block_picks, out_weight, out_grad):
    query_rows = queries[0]
    key_rows = key_states[0]
    value_rows = value_states[0]
    grad_rows = out_grad[0]
    picks_here = block_picks[0]
    tok_count = query_rows.shape[0]
    q_cols = query_rows.shape[1]
    kv_cols = key_rows.shape[1]
    kv_count = kv_cols // HEAD_DIM
    group_size = q_cols // kv_cols
    score_scale = 1.0 / math.sqrt(HEAD_DIM)
    seq_count = lax.axis_size("seq")
    level_count = seq_count.bit_length() - 1
    shard_index = lax.axis_index("seq")
    far_keys = []
    far_values = []
    for level_index in range(level_count):
        distance = 1 << level_index
        got_keys, got_values = shifted((key_rows, value_rows), "seq", distance)
        row_begin = picks_here[level_index, shard_index] * BLOCK
        far_keys.append(lax.dynamic_slice_in_dim(got_keys, row_begin, BLOCK, 0))
        far_values.append(lax.dynamic_slice_in_dim(got_values, row_begin, BLOCK, 0))
    all_keys = jnp.concatenate([key_rows] + far_keys, 0)
    all_values = jnp.concatenate([value_rows] + far_values, 0)
    key_total = all_keys.shape[0]
    row_ids = lax.broadcasted_iota(jnp.int32, (tok_count, key_total), 0)
    col_ids = lax.broadcasted_iota(jnp.int32, (tok_count, key_total), 1)
    far_level = jnp.maximum(col_ids - tok_count, 0) // BLOCK
    far_seen = shard_index >= jnp.left_shift(jnp.int32(1), far_level)
    visible = jnp.where(col_ids < tok_count, col_ids <= row_ids, far_seen)
    whole_weight = lax.all_gather(out_weight, ("dp", "seq"), axis=0, tiled=True)
    attn_grad = lax.dot_general(
        grad_rows, whole_weight, (((1,), (1,)), ((), ())), preferred_element_type=jnp.float32
    )
    attn_grad = attn_grad.astype(jnp.bfloat16)
    query_heads = query_rows.reshape(tok_count, kv_count, group_size, HEAD_DIM)
    key_heads = all_keys.reshape(key_total, kv_count, HEAD_DIM)
    value_heads = all_values.reshape(key_total, kv_count, HEAD_DIM)
    grad_heads = attn_grad.reshape(tok_count, kv_count, group_size, HEAD_DIM)
    attn_parts = []
    dq_parts = []
    dk_parts = []
    dv_parts = []
    for group_index in range(kv_count):
        query_group = query_heads[:, group_index]
        key_group = key_heads[:, group_index]
        value_group = value_heads[:, group_index]
        grad_group = grad_heads[:, group_index]
        scores = (
            jnp.einsum("tgd,sd->gts", query_group, key_group, preferred_element_type=jnp.float32)
            * score_scale
        )
        scores = jnp.where(visible[None], scores, neg_fill)
        row_max = jnp.max(scores, axis=-1, keepdims=True)
        exp_scores = jnp.exp(scores - row_max)
        probs = exp_scores / jnp.sum(exp_scores, axis=-1, keepdims=True)
        probs_low = probs.astype(jnp.bfloat16)
        attn_group = jnp.einsum(
            "gts,sd->tgd", probs_low, value_group, preferred_element_type=jnp.float32
        ).astype(jnp.bfloat16)
        row_delta = jnp.einsum(
            "tgd,tgd->gt", grad_group, attn_group, preferred_element_type=jnp.float32
        )[:, :, None]
        prob_grad = jnp.einsum(
            "tgd,sd->gts", grad_group, value_group, preferred_element_type=jnp.float32
        )
        score_low = (probs * (prob_grad - row_delta)).astype(jnp.bfloat16)
        dq_parts.append(
            (
                jnp.einsum("gts,sd->tgd", score_low, key_group, preferred_element_type=jnp.float32)
                * score_scale
            ).astype(jnp.bfloat16)
        )
        dk_parts.append(
            jnp.einsum("gts,tgd->sd", score_low, query_group, preferred_element_type=jnp.float32)
            * score_scale
        )
        dv_parts.append(
            jnp.einsum("gts,tgd->sd", probs_low, grad_group, preferred_element_type=jnp.float32)
        )
        attn_parts.append(attn_group)
    attn_all = jnp.stack(attn_parts, 1).reshape(tok_count, q_cols)
    query_grad = jnp.stack(dq_parts, 1).reshape(tok_count, q_cols)
    key_terms = jnp.stack(dk_parts, 1).reshape(key_total, kv_cols)
    value_terms = jnp.stack(dv_parts, 1).reshape(key_total, kv_cols)
    layer_sum = jnp.dot(attn_all, whole_weight, preferred_element_type=jnp.float32)
    layer_out = layer_sum.astype(jnp.bfloat16)
    key_grad = key_terms[:tok_count]
    value_grad = value_terms[:tok_count]
    for level_index in range(level_count):
        distance = 1 << level_index
        begin = tok_count + level_index * BLOCK
        back_keys, back_values = shifted(
            (key_terms[begin : begin + BLOCK], value_terms[begin : begin + BLOCK]), "seq", -distance
        )
        source = jnp.minimum(shard_index + distance, seq_count - 1)
        row_begin = picks_here[level_index, source] * BLOCK
        key_grad = lax.dynamic_update_slice_in_dim(
            key_grad,
            lax.dynamic_slice_in_dim(key_grad, row_begin, BLOCK, 0) + back_keys,
            row_begin,
            0,
        )
        value_grad = lax.dynamic_update_slice_in_dim(
            value_grad,
            lax.dynamic_slice_in_dim(value_grad, row_begin, BLOCK, 0) + back_values,
            row_begin,
            0,
        )
    return (
        layer_out[None],
        query_grad[None],
        key_grad.astype(jnp.bfloat16)[None],
        value_grad.astype(jnp.bfloat16)[None],
    )


MESH = pl.DeviceIdType.MESH
NT = (((1,), (1,)), ((), ()))
NN = (((1,), (0,)), ((), ()))
TN = (((0,), (0,)), ((), ()))


def dot(a, b, dims):
    return lax.dot_general(a, b, dims, preferred_element_type=jnp.float32)


def fused_kernel(
    picks, q_hbm, k_in, v_in, w_in, og_hbm,
    lo_out, dq_out, dk_out, dv_out,
    q_v, og_v, wbuf, kv_all, k_t, v_t, kv_stage, probs, attn_t, lo_acc,
    dk_acc, dv_acc, gr_stage, gr_in,
    in_sem, kv_ssem, kv_rsem, z_ssem, x_ssem, y_ssem, s_ssem, xh_ssem, yh_ssem,
    z_rsem, x_rsem, y_rsem, s_rsem, xh_rsem, yh_rsem, gr_ssem, gr_rsem,
):
    dp = lax.axis_index("dp")
    seq = lax.axis_index("seq")
    n_seq = lax.axis_size("seq")
    n_z = n_seq // 2
    x, core = dp // 2, dp % 2
    z, y = seq // 2, seq % 2
    rows = w_in.shape[0]
    half = rows // 2
    tok = q_v.shape[0]
    group_rows = rows * n_seq
    pair_rows = group_rows // 2
    heads = q_v.shape[1] // HEAD_DIM
    kv_heads = k_in.shape[1] // HEAD_DIM
    group_size = heads // kv_heads
    pair_heads = group_size // 2
    levels = n_seq.bit_length() - 1
    scale = 1.0 / math.sqrt(HEAD_DIM)
    log2_scale = scale * math.log2(math.e)

    sib = (x * 2 + 1 - core, seq)
    xn = ((1 - x) * 2 + core, seq)
    yn = (dp, z * 2 + 1 - y)
    d_own, d_sib, d_x, d_xs = dp, sib[0], xn[0], (1 - x) * 2 + 1 - core

    q_copy = pltpu.make_async_copy(q_hbm, q_v, in_sem.at[0])
    og_copy = pltpu.make_async_copy(og_hbm, og_v, in_sem.at[1])
    q_copy.start()
    og_copy.start()

    barrier = pltpu.get_barrier_semaphore()
    count = jnp.int32(2)
    for dev in (sib, xn):
        pl.semaphore_signal(barrier, inc=1, device_id=dev, device_id_type=MESH)
    for j in range(levels):
        dist = 1 << j

        @pl.when(seq + dist < n_seq)
        def _():
            pl.semaphore_signal(barrier, inc=1, device_id=(dp, seq + dist), device_id_type=MESH)

        @pl.when(seq >= dist)
        def _():
            pl.semaphore_signal(barrier, inc=1, device_id=(dp, seq - dist), device_id_type=MESH)

        count += (seq + dist < n_seq).astype(jnp.int32) + (seq >= dist).astype(jnp.int32)

    def w_row(d, zz, yy):
        return pl.multiple_of((d * n_seq + zz * 2 + yy) * rows, rows)

    def w_at(d, zz, yy):
        return wbuf.at[pl.ds(w_row(d, zz, yy), rows)]

    def w_half(d, zz, yy, hf):
        return wbuf.at[pl.ds(pl.multiple_of(w_row(d, zz, yy) + hf * half, half), half)]

    def stage_group(g):
        cols = group_cols(g)
        for j in range(levels):
            second = picks[0, j, jnp.minimum(seq + (1 << j), n_seq - 1)].astype(jnp.float32)
            for i, buf in enumerate((k_in, v_in)):
                first_rows = buf[0:BLOCK, cols].astype(jnp.float32) * (1.0 - second)
                second_rows = buf[BLOCK : 2 * BLOCK, cols].astype(jnp.float32) * second
                kv_stage[g, j, i] = (first_rows + second_rows).astype(jnp.bfloat16)

    def group_cols(g):
        return pl.ds(pl.multiple_of(g * HEAD_DIM, HEAD_DIM), HEAD_DIM)

    stage_group(d_own)
    wbuf[pl.ds(w_row(dp, z, y), rows), :] = w_in[...]
    pl.semaphore_wait(barrier, count)

    def remote(src, dst, ssem, rsem, dev):
        return pltpu.make_async_remote_copy(
            src_ref=src, dst_ref=dst, send_sem=ssem, recv_sem=rsem, device_id=dev, device_id_type=MESH
        )

    def kv_copy(g, j):
        dst = kv_all.at[g, :, pl.ds(tok + j * BLOCK, BLOCK)]
        dev = (dp, jnp.minimum(seq + (1 << j), n_seq - 1))
        return remote(kv_stage.at[g, j], dst, kv_ssem.at[g, j], kv_rsem.at[g, j], dev)

    def kv_send(g):
        for j in range(levels):
            @pl.when(seq + (1 << j) < n_seq)
            def _():
                kv_copy(g, j).start()

    z_order = (z, jnp.bitwise_xor(z, 1), jnp.where(z < 2, 2, 1), jnp.where(z < 2, 3, 0))

    def z_copy(zz, up):
        dev = (dp, seq + 2) if up else (dp, seq - 2)
        return remote(w_at(dp, zz, y), w_at(dp, zz, y), z_ssem.at[int(up), zz], z_rsem.at[zz], dev)

    def x_copy(zz, d):
        return remote(w_at(d, zz, y), w_at(d, zz, y), x_ssem.at[zz], x_rsem.at[zz], xn)

    def y_copy(zz, yy):
        return remote(w_at(dp, zz, yy), w_at(dp, zz, yy), y_ssem.at[zz], y_rsem.at[zz], yn)

    def xh_copy(zz, d):
        piece = w_half(d, zz, 1 - y, 1)
        return remote(piece, piece, xh_ssem.at[zz], xh_rsem.at[zz], xn)

    def yh_copy(zz, yy):
        piece = w_half(d_x, zz, yy, 0)
        return remote(piece, piece, yh_ssem.at[zz], yh_rsem.at[zz], yn)

    def s_copy(zz, kind, other):
        d = (d_x if kind & 1 else d_own) if not other else (d_xs if kind & 1 else d_sib)
        yy = 1 - y if kind & 2 else y
        piece = w_at(d, zz, yy)
        return remote(piece, piece, s_ssem.at[kind, zz], s_rsem.at[kind, zz], sib)

    def z_sends(zz, act):
        @pl.when(jnp.logical_and(zz <= z, z < n_z - 1))
        def _():
            act(z_copy(zz, True))

        @pl.when(jnp.logical_and(zz >= z, z > 0))
        def _():
            act(z_copy(zz, False))

    def start(c):
        c.start()

    def own_event(i):
        zz = z_order[i]
        if i:
            z_copy(zz, True).wait_recv()
        z_sends(zz, start)
        x_copy(zz, d_own).start()
        y_copy(zz, y).start()
        s_copy(zz, 0, False).start()

    def xy_event(i):
        zz = z_order[i]
        x_copy(zz, d_x).wait_recv()
        yh_copy(zz, y).start()
        s_copy(zz, 1, False).start()
        y_copy(zz, 1 - y).wait_recv()
        xh_copy(zz, d_own).start()
        s_copy(zz, 2, False).start()

    def diag_event(i):
        zz = z_order[i]
        yh_copy(zz, 1 - y).wait_recv()
        xh_copy(zz, d_x).wait_recv()
        s_copy(zz, 3, False).start()

    def sib_wait(i, kinds):
        for kind in kinds:
            s_copy(z_order[i], kind, True).wait_recv()

    kv_send(d_own)
    own_event(0)
    for g in (d_sib, d_x, d_xs):
        stage_group(g)

    for j in range(levels):
        @pl.when(seq < (1 << j))
        def _():
            block = slice(tok + j * BLOCK, tok + (j + 1) * BLOCK)
            kv_all[:, :, block, :] = jnp.zeros((kv_heads, 2, BLOCK, HEAD_DIM), kv_all.dtype)

    for g in range(kv_heads):
        for i, buf in enumerate((k_in, v_in)):
            kv_all[g, i, 0:tok, :] = buf[:, g * HEAD_DIM : (g + 1) * HEAD_DIM]
    dk_acc[...] = jnp.zeros_like(dk_acc)
    dv_acc[...] = jnp.zeros_like(dv_acc)
    lo_acc[...] = jnp.zeros_like(lo_acc)
    q_copy.wait()

    causal = lax.broadcasted_iota(jnp.int32, (tok, tok), 0) <= lax.broadcasted_iota(jnp.int32, (tok, tok), 1)

    def softmax_head(h, carry):
        g = h // group_size
        s = dot(kv_all[g, 0], q_v[:, group_cols(h)], NT)
        parts = [jnp.where(causal, s[:tok], neg_fill)]
        for j in range(levels):
            bias = jnp.where(seq >= (1 << j), 0.0, neg_fill).astype(jnp.float32)
            parts.append(s[tok + j * BLOCK : tok + (j + 1) * BLOCK] + bias)
        top = jnp.max(parts[0], axis=0, keepdims=True)
        for part in parts[1:]:
            top = jnp.maximum(top, jnp.max(part, axis=0, keepdims=True))
        exps = [jnp.exp2((part - top) * log2_scale) for part in parts]
        total = jnp.sum(exps[0], axis=0, keepdims=True)
        for part in exps[1:]:
            total = total + jnp.sum(part, axis=0, keepdims=True)
        inv = 1.0 / total
        low = jnp.concatenate([(part * inv).astype(jnp.bfloat16) for part in exps], 0)
        probs[h] = low
        at = dot(v_t[g], low, NN)
        attn_t[pl.ds(pl.multiple_of(h * HEAD_DIM, HEAD_DIM), HEAD_DIM), :] = at.astype(jnp.bfloat16)
        return carry

    def softmaxes(g):
        for j in range(levels):
            @pl.when(seq >= (1 << j))
            def _():
                kv_copy(g, j).wait_recv()

        k_t[g] = kv_all[g, 0].T
        v_t[g] = kv_all[g, 1].T
        lax.fori_loop(g * group_size, (g + 1) * group_size, softmax_head, 0)

    def unit(g, p):
        base = pl.multiple_of(g * group_rows + p * pair_rows, pair_rows)
        wp = wbuf[pl.ds(base, pair_rows), :]
        g_t = dot(wp, og_v[...], NT).astype(jnp.bfloat16)
        a_t = attn_t[pl.ds(base, pair_rows), :]
        lo_acc[...] += dot(a_t, wp, TN)
        dk = dk_acc[g]
        dv = dv_acc[g]
        for i in range(pair_heads):
            h = g * group_size + p * pair_heads + i
            gh = g_t[i * HEAD_DIM : (i + 1) * HEAD_DIM]
            ah = a_t[i * HEAD_DIM : (i + 1) * HEAD_DIM]
            delta = jnp.sum(gh.astype(jnp.float32) * ah.astype(jnp.float32), axis=0, keepdims=True)
            low = probs[h]
            dprob = dot(kv_all[g, 1], gh, NN)
            ds = (low.astype(jnp.float32) * (dprob - delta)).astype(jnp.bfloat16)
            dq_t = dot(k_t[g], ds, NN) * scale
            dq_out[:, group_cols(h)] = dq_t.T.astype(jnp.bfloat16)
            dk += dot(ds, q_v[:, group_cols(h)], NN)
            dv += dot(low, gh, NT)
        dk_acc[g] = dk
        dv_acc[g] = dv

    def gr_copy(g, j, back):
        dev = (dp, jnp.maximum(seq - (1 << j), 0))
        return remote(gr_stage.at[g, j], gr_in.at[g, j], gr_ssem.at[g, j], gr_rsem.at[g, j], dev)

    def send_grads(g):
        for j in range(levels):
            @pl.when(seq >= (1 << j))
            def _():
                begin = tok + j * BLOCK
                gr_stage[g, j, 0] = (dk_acc[g, begin : begin + BLOCK, :] * scale).astype(jnp.bfloat16)
                gr_stage[g, j, 1] = dv_acc[g, begin : begin + BLOCK, :].astype(jnp.bfloat16)
                gr_copy(g, j, True).start()

    def finish_grads(g):
        cols = group_cols(g)
        for j in range(levels):
            @pl.when(seq + (1 << j) < n_seq)
            def _():
                gr_copy(g, j, True).wait_recv()
                second = picks[0, j, jnp.minimum(seq + (1 << j), n_seq - 1)].astype(jnp.float32)
                for b, here in enumerate((1.0 - second, second)):
                    part = slice(b * BLOCK, (b + 1) * BLOCK)
                    dk_acc[g, part, :] += gr_in[g, j, 0].astype(jnp.float32) * (here * math.sqrt(HEAD_DIM))
                    dv_acc[g, part, :] += gr_in[g, j, 1].astype(jnp.float32) * here

        dk_out[:, cols] = (dk_acc[g, 0:tok, :] * scale).astype(jnp.bfloat16)
        dv_out[:, cols] = dv_acc[g, 0:tok, :].astype(jnp.bfloat16)

    p0 = z // 2
    p1 = 1 - p0
    own_event(1)
    xy_event(0)
    kv_send(d_sib)
    softmaxes(d_own)
    own_event(2)
    xy_event(1)
    kv_send(d_x)
    diag_event(0)
    og_copy.wait()
    unit(d_own, p0)
    own_event(3)
    xy_event(2)
    kv_send(d_xs)
    diag_event(1)
    softmaxes(d_sib)
    for i in (0, 1):
        sib_wait(i, (0, 2))
    unit(d_sib, p0)
    xy_event(3)
    diag_event(2)
    unit(d_own, p1)
    send_grads(d_own)
    for i in (2, 3):
        sib_wait(i, (0, 2))
    unit(d_sib, p1)
    send_grads(d_sib)
    softmaxes(d_x)
    unit(d_x, p0)
    diag_event(3)
    softmaxes(d_xs)
    unit(d_x, p1)
    send_grads(d_x)
    for i in range(n_z):
        sib_wait(i, (1, 3))
    unit(d_xs, p0)
    unit(d_xs, p1)
    send_grads(d_xs)
    lo_out[...] = lo_acc[...].astype(jnp.bfloat16)
    for g in (d_own, d_sib, d_x, d_xs):
        finish_grads(g)

    def done(c):
        c.wait_send()

    for i in range(n_z):
        zz = z_order[i]
        z_sends(zz, done)
        x_copy(zz, d_own).wait_send()
        y_copy(zz, y).wait_send()
        yh_copy(zz, y).wait_send()
        xh_copy(zz, d_own).wait_send()
        for kind in range(4):
            s_copy(zz, kind, False).wait_send()
    for j in range(levels):
        @pl.when(seq + (1 << j) < n_seq)
        def _():
            for g in range(kv_heads):
                kv_copy(g, j).wait_send()

        @pl.when(seq >= (1 << j))
        def _():
            for g in range(kv_heads):
                gr_copy(g, j, True).wait_send()


def fused_shards(queries, key_states, value_states, block_picks, out_weight, out_grad):
    q, k, v, og = queries[0], key_states[0], value_states[0], out_grad[0]
    tok, q_cols = q.shape
    kv_cols = k.shape[1]
    n_seq = lax.axis_size("seq")
    levels = n_seq.bit_length() - 1
    keys = tok + levels * BLOCK
    heads, kv_heads = q_cols // HEAD_DIM, kv_cols // HEAD_DIM
    out_width = out_weight.shape[1]
    n_z = n_seq // 2
    vmem = pl.BlockSpec(memory_space=pltpu.VMEM)
    hbm = pl.BlockSpec(memory_space=pl.ANY)
    smem = pl.BlockSpec(memory_space=pltpu.SMEM)
    low = jnp.bfloat16
    dma = pltpu.SemaphoreType.DMA
    outs = pl.pallas_call(
        fused_kernel,
        out_shape=(
            jax.ShapeDtypeStruct((tok, out_width), low),
            jax.ShapeDtypeStruct((tok, q_cols), low),
            jax.ShapeDtypeStruct((tok, kv_cols), low),
            jax.ShapeDtypeStruct((tok, kv_cols), low),
        ),
        in_specs=[smem, hbm, vmem, vmem, vmem, hbm],
        out_specs=(vmem, vmem, vmem, vmem),
        scratch_shapes=[
            pltpu.VMEM((tok, q_cols), low),
            pltpu.VMEM((tok, out_width), low),
            pltpu.VMEM((q_cols, out_width), low),
            pltpu.VMEM((kv_heads, 2, keys, HEAD_DIM), low),
            pltpu.VMEM((kv_heads, HEAD_DIM, keys), low),
            pltpu.VMEM((kv_heads, HEAD_DIM, keys), low),
            pltpu.VMEM((kv_heads, levels, 2, BLOCK, HEAD_DIM), low),
            pltpu.VMEM((heads, keys, tok), low),
            pltpu.VMEM((q_cols, tok), low),
            pltpu.VMEM((tok, out_width), jnp.float32),
            pltpu.VMEM((kv_heads, keys, HEAD_DIM), jnp.float32),
            pltpu.VMEM((kv_heads, keys, HEAD_DIM), jnp.float32),
            pltpu.VMEM((kv_heads, levels, 2, BLOCK, HEAD_DIM), low),
            pltpu.VMEM((kv_heads, levels, 2, BLOCK, HEAD_DIM), low),
            dma((2,)),
            dma((kv_heads, levels)),
            dma((kv_heads, levels)),
            dma((2, n_z)),
            dma((n_z,)),
            dma((n_z,)),
            dma((4, n_z)),
            dma((n_z,)),
            dma((n_z,)),
            dma((n_z,)),
            dma((n_z,)),
            dma((n_z,)),
            dma((4, n_z)),
            dma((n_z,)),
            dma((n_z,)),
            dma((kv_heads, levels)),
            dma((kv_heads, levels)),
        ],
        compiler_params=pltpu.CompilerParams(
            collective_id=0, has_side_effects=True, vmem_limit_bytes=56 * 1024 * 1024
        ),
    )(block_picks, q, k, v, out_weight, og)
    return tuple(out[None] for out in outs)


def solution(mesh):
    fused = mesh.shape["dp"] == 4 and mesh.shape["seq"] == 8
    return jax.shard_map(
        fused_shards if fused else shards,
        mesh=mesh,
        in_specs=(
            P("dp", "seq", None),
            P("dp", "seq", None),
            P("dp", "seq", None),
            P("dp", None, None),
            P(("dp", "seq"), None),
            P("dp", "seq", None),
        ),
        out_specs=(
            P("dp", "seq", None),
            P("dp", "seq", None),
            P("dp", "seq", None),
            P("dp", "seq", None),
        ),
        check_vma=False,
    )
```

```python
import math

import jax
import jax.numpy as jnp
from jax import lax
from jax.experimental import pallas as pl
from jax.experimental.pallas import tpu as pltpu
from jax.sharding import PartitionSpec as P

HEAD_DIM = 128
BLOCK = 128


neg_fill = -1e30


def shifted(block, axis, distance):
    devices = range(lax.axis_size(axis))
    route = [(i - distance, i) for i in devices if i - distance in devices]
    return lax.ppermute(block, axis, route)


def shards(queries, key_states, value_states, block_picks, out_weight, out_grad):
    query_rows = queries[0]
    key_rows = key_states[0]
    value_rows = value_states[0]
    grad_rows = out_grad[0]
    picks_here = block_picks[0]
    tok_count = query_rows.shape[0]
    q_cols = query_rows.shape[1]
    kv_cols = key_rows.shape[1]
    kv_count = kv_cols // HEAD_DIM
    group_size = q_cols // kv_cols
    score_scale = 1.0 / math.sqrt(HEAD_DIM)
    seq_count = lax.axis_size("seq")
    level_count = seq_count.bit_length() - 1
    shard_index = lax.axis_index("seq")
    far_keys = []
    far_values = []
    for level_index in range(level_count):
        distance = 1 << level_index
        got_keys, got_values = shifted((key_rows, value_rows), "seq", distance)
        row_begin = picks_here[level_index, shard_index] * BLOCK
        far_keys.append(lax.dynamic_slice_in_dim(got_keys, row_begin, BLOCK, 0))
        far_values.append(lax.dynamic_slice_in_dim(got_values, row_begin, BLOCK, 0))
    all_keys = jnp.concatenate([key_rows] + far_keys, 0)
    all_values = jnp.concatenate([value_rows] + far_values, 0)
    key_total = all_keys.shape[0]
    row_ids = lax.broadcasted_iota(jnp.int32, (tok_count, key_total), 0)
    col_ids = lax.broadcasted_iota(jnp.int32, (tok_count, key_total), 1)
    far_level = jnp.maximum(col_ids - tok_count, 0) // BLOCK
    far_seen = shard_index >= jnp.left_shift(jnp.int32(1), far_level)
    visible = jnp.where(col_ids < tok_count, col_ids <= row_ids, far_seen)
    whole_weight = lax.all_gather(out_weight, ("dp", "seq"), axis=0, tiled=True)
    attn_grad = lax.dot_general(
        grad_rows, whole_weight, (((1,), (1,)), ((), ())), preferred_element_type=jnp.float32
    )
    attn_grad = attn_grad.astype(jnp.bfloat16)
    query_heads = query_rows.reshape(tok_count, kv_count, group_size, HEAD_DIM)
    key_heads = all_keys.reshape(key_total, kv_count, HEAD_DIM)
    value_heads = all_values.reshape(key_total, kv_count, HEAD_DIM)
    grad_heads = attn_grad.reshape(tok_count, kv_count, group_size, HEAD_DIM)
    attn_parts = []
    dq_parts = []
    dk_parts = []
    dv_parts = []
    for group_index in range(kv_count):
        query_group = query_heads[:, group_index]
        key_group = key_heads[:, group_index]
        value_group = value_heads[:, group_index]
        grad_group = grad_heads[:, group_index]
        scores = (
            jnp.einsum("tgd,sd->gts", query_group, key_group, preferred_element_type=jnp.float32)
            * score_scale
        )
        scores = jnp.where(visible[None], scores, neg_fill)
        row_max = jnp.max(scores, axis=-1, keepdims=True)
        exp_scores = jnp.exp(scores - row_max)
        probs = exp_scores / jnp.sum(exp_scores, axis=-1, keepdims=True)
        probs_low = probs.astype(jnp.bfloat16)
        attn_group = jnp.einsum(
            "gts,sd->tgd", probs_low, value_group, preferred_element_type=jnp.float32
        ).astype(jnp.bfloat16)
        row_delta = jnp.einsum(
            "tgd,tgd->gt", grad_group, attn_group, preferred_element_type=jnp.float32
        )[:, :, None]
        prob_grad = jnp.einsum(
            "tgd,sd->gts", grad_group, value_group, preferred_element_type=jnp.float32
        )
        score_low = (probs * (prob_grad - row_delta)).astype(jnp.bfloat16)
        dq_parts.append(
            (
                jnp.einsum("gts,sd->tgd", score_low, key_group, preferred_element_type=jnp.float32)
                * score_scale
            ).astype(jnp.bfloat16)
        )
        dk_parts.append(
            jnp.einsum("gts,tgd->sd", score_low, query_group, preferred_element_type=jnp.float32)
            * score_scale
        )
        dv_parts.append(
            jnp.einsum("gts,tgd->sd", probs_low, grad_group, preferred_element_type=jnp.float32)
        )
        attn_parts.append(attn_group)
    attn_all = jnp.stack(attn_parts, 1).reshape(tok_count, q_cols)
    query_grad = jnp.stack(dq_parts, 1).reshape(tok_count, q_cols)
    key_terms = jnp.stack(dk_parts, 1).reshape(key_total, kv_cols)
    value_terms = jnp.stack(dv_parts, 1).reshape(key_total, kv_cols)
    layer_sum = jnp.dot(attn_all, whole_weight, preferred_element_type=jnp.float32)
    layer_out = layer_sum.astype(jnp.bfloat16)
    key_grad = key_terms[:tok_count]
    value_grad = value_terms[:tok_count]
    for level_index in range(level_count):
        distance = 1 << level_index
        begin = tok_count + level_index * BLOCK
        back_keys, back_values = shifted(
            (key_terms[begin : begin + BLOCK], value_terms[begin : begin + BLOCK]), "seq", -distance
        )
        source = jnp.minimum(shard_index + distance, seq_count - 1)
        row_begin = picks_here[level_index, source] * BLOCK
        key_grad = lax.dynamic_update_slice_in_dim(
            key_grad,
            lax.dynamic_slice_in_dim(key_grad, row_begin, BLOCK, 0) + back_keys,
            row_begin,
            0,
        )
        value_grad = lax.dynamic_update_slice_in_dim(
            value_grad,
            lax.dynamic_slice_in_dim(value_grad, row_begin, BLOCK, 0) + back_values,
            row_begin,
            0,
        )
    return (
        layer_out[None],
        query_grad[None],
        key_grad.astype(jnp.bfloat16)[None],
        value_grad.astype(jnp.bfloat16)[None],
    )


MESH = pl.DeviceIdType.MESH
NT = (((1,), (1,)), ((), ()))
NN = (((1,), (0,)), ((), ()))
TN = (((0,), (0,)), ((), ()))


def dot(a, b, dims):
    return lax.dot_general(a, b, dims, preferred_element_type=jnp.float32)


def fused_kernel(
    picks, q_hbm, k_in, v_in, w_in, og_hbm,
    lo_out, dq_out, dk_out, dv_out,
    q_v, og_v, wbuf, kv_all, k_t, v_t, kv_stage, probs, attn_t, lo_acc,
    dk_acc, dv_acc, gr_stage, gr_in,
    in_sem, kv_ssem, kv_rsem, z_ssem, x_ssem, y_ssem, s_ssem, xh_ssem, yh_ssem,
    z_rsem, x_rsem, y_rsem, s_rsem, xh_rsem, yh_rsem, gr_ssem, gr_rsem,
):
    dp = lax.axis_index("dp")
    seq = lax.axis_index("seq")
    n_seq = lax.axis_size("seq")
    n_z = n_seq // 2
    x, core = dp // 2, dp % 2
    z, y = seq // 2, seq % 2
    rows = w_in.shape[0]
    half = rows // 2
    tok = q_v.shape[0]
    group_rows = rows * n_seq
    pair_rows = group_rows // 2
    heads = q_v.shape[1] // HEAD_DIM
    kv_heads = k_in.shape[1] // HEAD_DIM
    group_size = heads // kv_heads
    pair_heads = group_size // 2
    levels = n_seq.bit_length() - 1
    scale = 1.0 / math.sqrt(HEAD_DIM)
    log2_scale = scale * math.log2(math.e)

    sib = (x * 2 + 1 - core, seq)
    xn = ((1 - x) * 2 + core, seq)
    yn = (dp, z * 2 + 1 - y)
    d_own, d_sib, d_x, d_xs = dp, sib[0], xn[0], (1 - x) * 2 + 1 - core

    q_copy = pltpu.make_async_copy(q_hbm, q_v, in_sem.at[0])
    og_copy = pltpu.make_async_copy(og_hbm, og_v, in_sem.at[1])
    q_copy.start()
    og_copy.start()

    barrier = pltpu.get_barrier_semaphore()
    count = jnp.int32(2)
    for dev in (sib, xn):
        pl.semaphore_signal(barrier, inc=1, device_id=dev, device_id_type=MESH)
    for j in range(levels):
        dist = 1 << j

        @pl.when(seq + dist < n_seq)
        def _():
            pl.semaphore_signal(barrier, inc=1, device_id=(dp, seq + dist), device_id_type=MESH)

        @pl.when(seq >= dist)
        def _():
            pl.semaphore_signal(barrier, inc=1, device_id=(dp, seq - dist), device_id_type=MESH)

        count += (seq + dist < n_seq).astype(jnp.int32) + (seq >= dist).astype(jnp.int32)

    def w_row(d, zz, yy):
        return pl.multiple_of((d * n_seq + zz * 2 + yy) * rows, rows)

    def w_at(d, zz, yy):
        return wbuf.at[pl.ds(w_row(d, zz, yy), rows)]

    def w_half(d, zz, yy, hf):
        return wbuf.at[pl.ds(pl.multiple_of(w_row(d, zz, yy) + hf * half, half), half)]

    def stage_group(g):
        cols = group_cols(g)
        for j in range(levels):
            second = picks[0, j, jnp.minimum(seq + (1 << j), n_seq - 1)].astype(jnp.float32)
            for i, buf in enumerate((k_in, v_in)):
                first_rows = buf[0:BLOCK, cols].astype(jnp.float32) * (1.0 - second)
                second_rows = buf[BLOCK : 2 * BLOCK, cols].astype(jnp.float32) * second
                kv_stage[g, j, i] = (first_rows + second_rows).astype(jnp.bfloat16)

    def group_cols(g):
        return pl.ds(pl.multiple_of(g * HEAD_DIM, HEAD_DIM), HEAD_DIM)

    stage_group(d_own)
    wbuf[pl.ds(w_row(dp, z, y), rows), :] = w_in[...]
    pl.semaphore_wait(barrier, count)

    def remote(src, dst, ssem, rsem, dev):
        return pltpu.make_async_remote_copy(
            src_ref=src, dst_ref=dst, send_sem=ssem, recv_sem=rsem, device_id=dev, device_id_type=MESH
        )

    def kv_copy(g, j):
        dst = kv_all.at[g, :, pl.ds(tok + j * BLOCK, BLOCK)]
        dev = (dp, jnp.minimum(seq + (1 << j), n_seq - 1))
        return remote(kv_stage.at[g, j], dst, kv_ssem.at[g, j], kv_rsem.at[g, j], dev)

    def kv_send(g):
        for j in range(levels):
            @pl.when(seq + (1 << j) < n_seq)
            def _():
                kv_copy(g, j).start()

    z_order = (z, jnp.bitwise_xor(z, 1), jnp.where(z < 2, 2, 1), jnp.where(z < 2, 3, 0))

    def z_copy(zz, up):
        dev = (dp, seq + 2) if up else (dp, seq - 2)
        return remote(w_at(dp, zz, y), w_at(dp, zz, y), z_ssem.at[int(up), zz], z_rsem.at[zz], dev)

    def x_copy(zz, d):
        return remote(w_at(d, zz, y), w_at(d, zz, y), x_ssem.at[zz], x_rsem.at[zz], xn)

    def y_copy(zz, yy):
        return remote(w_at(dp, zz, yy), w_at(dp, zz, yy), y_ssem.at[zz], y_rsem.at[zz], yn)

    def xh_copy(zz, d):
        piece = w_half(d, zz, 1 - y, 1)
        return remote(piece, piece, xh_ssem.at[zz], xh_rsem.at[zz], xn)

    def yh_copy(zz, yy):
        piece = w_half(d_x, zz, yy, 0)
        return remote(piece, piece, yh_ssem.at[zz], yh_rsem.at[zz], yn)

    def s_copy(zz, kind, other):
        d = (d_x if kind & 1 else d_own) if not other else (d_xs if kind & 1 else d_sib)
        yy = 1 - y if kind & 2 else y
        piece = w_at(d, zz, yy)
        return remote(piece, piece, s_ssem.at[kind, zz], s_rsem.at[kind, zz], sib)

    def z_sends(zz, act):
        @pl.when(jnp.logical_and(zz <= z, z < n_z - 1))
        def _():
            act(z_copy(zz, True))

        @pl.when(jnp.logical_and(zz >= z, z > 0))
        def _():
            act(z_copy(zz, False))

    def start(c):
        c.start()

    def own_event(i):
        zz = z_order[i]
        if i:
            z_copy(zz, True).wait_recv()
        z_sends(zz, start)
        x_copy(zz, d_own).start()
        y_copy(zz, y).start()
        s_copy(zz, 0, False).start()

    def xy_event(i):
        zz = z_order[i]
        x_copy(zz, d_x).wait_recv()
        s_copy(zz, 1, False).start()
        y_copy(zz, 1 - y).wait_recv()
        s_copy(zz, 2, False).start()

    def half_event(i):
        yh_copy(z_order[i], y).start()
        xh_copy(z_order[i], d_own).start()

    def diag_event(i):
        zz = z_order[i]
        yh_copy(zz, 1 - y).wait_recv()
        xh_copy(zz, d_x).wait_recv()
        s_copy(zz, 3, False).start()

    def sib_wait(i, kinds):
        for kind in kinds:
            s_copy(z_order[i], kind, True).wait_recv()

    kv_send(d_own)
    own_event(0)
    for g in (d_sib, d_x, d_xs):
        stage_group(g)

    for j in range(levels):
        @pl.when(seq < (1 << j))
        def _():
            block = slice(tok + j * BLOCK, tok + (j + 1) * BLOCK)
            kv_all[:, :, block, :] = jnp.zeros((kv_heads, 2, BLOCK, HEAD_DIM), kv_all.dtype)

    for g in range(kv_heads):
        for i, buf in enumerate((k_in, v_in)):
            kv_all[g, i, 0:tok, :] = buf[:, g * HEAD_DIM : (g + 1) * HEAD_DIM]
    dk_acc[...] = jnp.zeros_like(dk_acc)
    dv_acc[...] = jnp.zeros_like(dv_acc)
    lo_acc[...] = jnp.zeros_like(lo_acc)
    q_copy.wait()

    causal = lax.broadcasted_iota(jnp.int32, (tok, tok), 0) <= lax.broadcasted_iota(jnp.int32, (tok, tok), 1)

    def softmax_head(h, carry):
        g = h // group_size
        s = dot(kv_all[g, 0], q_v[:, group_cols(h)], NT)
        parts = [jnp.where(causal, s[:tok], neg_fill)]
        for j in range(levels):
            bias = jnp.where(seq >= (1 << j), 0.0, neg_fill).astype(jnp.float32)
            parts.append(s[tok + j * BLOCK : tok + (j + 1) * BLOCK] + bias)
        top = jnp.max(parts[0], axis=0, keepdims=True)
        for part in parts[1:]:
            top = jnp.maximum(top, jnp.max(part, axis=0, keepdims=True))
        exps = [jnp.exp2((part - top) * log2_scale) for part in parts]
        total = jnp.sum(exps[0], axis=0, keepdims=True)
        for part in exps[1:]:
            total = total + jnp.sum(part, axis=0, keepdims=True)
        inv = 1.0 / total
        low = jnp.concatenate([(part * inv).astype(jnp.bfloat16) for part in exps], 0)
        probs[h] = low
        at = dot(v_t[g], low, NN)
        attn_t[pl.ds(pl.multiple_of(h * HEAD_DIM, HEAD_DIM), HEAD_DIM), :] = at.astype(jnp.bfloat16)
        return carry

    def softmaxes(g):
        for j in range(levels):
            @pl.when(seq >= (1 << j))
            def _():
                kv_copy(g, j).wait_recv()

        k_t[g] = kv_all[g, 0].T
        v_t[g] = kv_all[g, 1].T
        lax.fori_loop(g * group_size, (g + 1) * group_size, softmax_head, 0)

    def unit(g, p):
        base = pl.multiple_of(g * group_rows + p * pair_rows, pair_rows)
        wp = wbuf[pl.ds(base, pair_rows), :]
        g_t = dot(wp, og_v[...], NT).astype(jnp.bfloat16)
        a_t = attn_t[pl.ds(base, pair_rows), :]
        lo_acc[...] += dot(a_t, wp, TN)
        dk = dk_acc[g]
        dv = dv_acc[g]
        for i in range(pair_heads):
            h = g * group_size + p * pair_heads + i
            gh = g_t[i * HEAD_DIM : (i + 1) * HEAD_DIM]
            ah = a_t[i * HEAD_DIM : (i + 1) * HEAD_DIM]
            delta = jnp.sum(gh.astype(jnp.float32) * ah.astype(jnp.float32), axis=0, keepdims=True)
            low = probs[h]
            dprob = dot(kv_all[g, 1], gh, NN)
            ds = (low.astype(jnp.float32) * (dprob - delta)).astype(jnp.bfloat16)
            dq_t = dot(k_t[g], ds, NN) * scale
            dq_out[:, group_cols(h)] = dq_t.T.astype(jnp.bfloat16)
            dk += dot(ds, q_v[:, group_cols(h)], NN)
            dv += dot(low, gh, NT)
        dk_acc[g] = dk
        dv_acc[g] = dv

    def gr_copy(g, j, back):
        dev = (dp, jnp.maximum(seq - (1 << j), 0))
        return remote(gr_stage.at[g, j], gr_in.at[g, j], gr_ssem.at[g, j], gr_rsem.at[g, j], dev)

    def send_grads(g):
        for j in range(levels):
            @pl.when(seq >= (1 << j))
            def _():
                begin = tok + j * BLOCK
                gr_stage[g, j, 0] = (dk_acc[g, begin : begin + BLOCK, :] * scale).astype(jnp.bfloat16)
                gr_stage[g, j, 1] = dv_acc[g, begin : begin + BLOCK, :].astype(jnp.bfloat16)
                gr_copy(g, j, True).start()

    def finish_grads(g):
        cols = group_cols(g)
        for j in range(levels):
            @pl.when(seq + (1 << j) < n_seq)
            def _():
                gr_copy(g, j, True).wait_recv()
                second = picks[0, j, jnp.minimum(seq + (1 << j), n_seq - 1)].astype(jnp.float32)
                for b, here in enumerate((1.0 - second, second)):
                    part = slice(b * BLOCK, (b + 1) * BLOCK)
                    dk_acc[g, part, :] += gr_in[g, j, 0].astype(jnp.float32) * (here * math.sqrt(HEAD_DIM))
                    dv_acc[g, part, :] += gr_in[g, j, 1].astype(jnp.float32) * here

        dk_out[:, cols] = (dk_acc[g, 0:tok, :] * scale).astype(jnp.bfloat16)
        dv_out[:, cols] = dv_acc[g, 0:tok, :].astype(jnp.bfloat16)

    p0 = z // 2
    p1 = 1 - p0
    own_event(1)
    xy_event(0)
    kv_send(d_sib)
    softmaxes(d_own)
    own_event(2)
    xy_event(1)
    kv_send(d_x)
    og_copy.wait()
    unit(d_own, p0)
    own_event(3)
    half_event(0)
    half_event(1)
    kv_send(d_xs)
    xy_event(2)
    half_event(2)
    xy_event(3)
    half_event(3)
    unit(d_own, p1)
    send_grads(d_own)
    softmaxes(d_sib)
    diag_event(0)
    for i in (0, 1):
        sib_wait(i, (0, 2))
    unit(d_sib, p0)
    diag_event(1)
    for i in (2, 3):
        sib_wait(i, (0, 2))
    unit(d_sib, p1)
    send_grads(d_sib)
    diag_event(2)
    softmaxes(d_x)
    unit(d_x, p0)
    diag_event(3)
    softmaxes(d_xs)
    unit(d_x, p1)
    send_grads(d_x)
    for i in range(n_z):
        sib_wait(i, (1, 3))
    unit(d_xs, p0)
    unit(d_xs, p1)
    send_grads(d_xs)
    lo_out[...] = lo_acc[...].astype(jnp.bfloat16)
    for g in (d_own, d_sib, d_x, d_xs):
        finish_grads(g)

    def done(c):
        c.wait_send()

    for i in range(n_z):
        zz = z_order[i]
        z_sends(zz, done)
        x_copy(zz, d_own).wait_send()
        y_copy(zz, y).wait_send()
        yh_copy(zz, y).wait_send()
        xh_copy(zz, d_own).wait_send()
        for kind in range(4):
            s_copy(zz, kind, False).wait_send()
    for j in range(levels):
        @pl.when(seq + (1 << j) < n_seq)
        def _():
            for g in range(kv_heads):
                kv_copy(g, j).wait_send()

        @pl.when(seq >= (1 << j))
        def _():
            for g in range(kv_heads):
                gr_copy(g, j, True).wait_send()


def fused_shards(queries, key_states, value_states, block_picks, out_weight, out_grad):
    q, k, v, og = queries[0], key_states[0], value_states[0], out_grad[0]
    tok, q_cols = q.shape
    kv_cols = k.shape[1]
    n_seq = lax.axis_size("seq")
    levels = n_seq.bit_length() - 1
    keys = tok + levels * BLOCK
    heads, kv_heads = q_cols // HEAD_DIM, kv_cols // HEAD_DIM
    out_width = out_weight.shape[1]
    n_z = n_seq // 2
    vmem = pl.BlockSpec(memory_space=pltpu.VMEM)
    hbm = pl.BlockSpec(memory_space=pl.ANY)
    smem = pl.BlockSpec(memory_space=pltpu.SMEM)
    low = jnp.bfloat16
    dma = pltpu.SemaphoreType.DMA
    outs = pl.pallas_call(
        fused_kernel,
        out_shape=(
            jax.ShapeDtypeStruct((tok, out_width), low),
            jax.ShapeDtypeStruct((tok, q_cols), low),
            jax.ShapeDtypeStruct((tok, kv_cols), low),
            jax.ShapeDtypeStruct((tok, kv_cols), low),
        ),
        in_specs=[smem, hbm, vmem, vmem, vmem, hbm],
        out_specs=(vmem, vmem, vmem, vmem),
        scratch_shapes=[
            pltpu.VMEM((tok, q_cols), low),
            pltpu.VMEM((tok, out_width), low),
            pltpu.VMEM((q_cols, out_width), low),
            pltpu.VMEM((kv_heads, 2, keys, HEAD_DIM), low),
            pltpu.VMEM((kv_heads, HEAD_DIM, keys), low),
            pltpu.VMEM((kv_heads, HEAD_DIM, keys), low),
            pltpu.VMEM((kv_heads, levels, 2, BLOCK, HEAD_DIM), low),
            pltpu.VMEM((heads, keys, tok), low),
            pltpu.VMEM((q_cols, tok), low),
            pltpu.VMEM((tok, out_width), jnp.float32),
            pltpu.VMEM((kv_heads, keys, HEAD_DIM), jnp.float32),
            pltpu.VMEM((kv_heads, keys, HEAD_DIM), jnp.float32),
            pltpu.VMEM((kv_heads, levels, 2, BLOCK, HEAD_DIM), low),
            pltpu.VMEM((kv_heads, levels, 2, BLOCK, HEAD_DIM), low),
            dma((2,)),
            dma((kv_heads, levels)),
            dma((kv_heads, levels)),
            dma((2, n_z)),
            dma((n_z,)),
            dma((n_z,)),
            dma((4, n_z)),
            dma((n_z,)),
            dma((n_z,)),
            dma((n_z,)),
            dma((n_z,)),
            dma((n_z,)),
            dma((4, n_z)),
            dma((n_z,)),
            dma((n_z,)),
            dma((kv_heads, levels)),
            dma((kv_heads, levels)),
        ],
        compiler_params=pltpu.CompilerParams(
            collective_id=0, has_side_effects=True, vmem_limit_bytes=56 * 1024 * 1024
        ),
    )(block_picks, q, k, v, out_weight, og)
    return tuple(out[None] for out in outs)


def solution(mesh):
    fused = mesh.shape["dp"] == 4 and mesh.shape["seq"] == 8
    return jax.shard_map(
        fused_shards if fused else shards,
        mesh=mesh,
        in_specs=(
            P("dp", "seq", None),
            P("dp", "seq", None),
            P("dp", "seq", None),
            P("dp", None, None),
            P(("dp", "seq"), None),
            P("dp", "seq", None),
        ),
        out_specs=(
            P("dp", "seq", None),
            P("dp", "seq", None),
            P("dp", "seq", None),
            P("dp", "seq", None),
        ),
        check_vma=False,
    )
```
